512 devices in a mesh: survey: 16 (over z, core), tile: 32 (over y, x).
Axes of the slice: x: 4, y: 8, z: 8, core: 2. Of those that a mesh axis runs over, the one named last changes fastest.
Arguments:
- data: bfloat16 [16, 256, 128, 256], P('survey', 'tile'), may hold values from -12 to 12
- correlation_index: int32 [16, 32, 16, 128], P(None, 'tile'), may hold values from 0 to 1023, as said below
- correlation_count: int32 [16, 32, 16], P(None, 'tile'), may hold values from 0 to 128, as said below
- smoothing: float32 [3], replicated, may hold values from 0.5 to 4
Outputs:
- fields: float32 [16, 3, 256, 128], P('survey', None, 'tile')
- volume: bfloat16 [16, 256, 128, 256], P('survey', 'tile')
The draws below stay inside these ranges and needn't reach their ends.
Inputs may be any that keep to these rules, and one draw needn't show every extreme that they name: `correlation_index`: each list holds 128 consecutive positions of the tile. `correlation_count`: zero where s equals p; one or more where s is p + 1 modulo 16; in every draw one tile and one destination group receive 128 live slots from every other group.
All inputs are finite; a program needn't handle non-finite values.
Results may differ from the reference program's by a relative error of at most 0.0014.
Values may be sent and summed in bfloat16 or wider, within the bound.
A program may use at most 64 MiB of HBM per device.

```python
import math
import jax
import jax.numpy as jnp
from jax import lax

TX = 8
TY = 128
NT = 256
CAP = 128
ROUNDS = 2
CG_ITERS = 3
SURVEYS = 16
TILES = 32
NXTOT = 256
N_TILE = 32


def time_smooth(raw_noise):
    tap_weights = (1.0, 2.0, 3.0, 2.0, 1.0)
    smoothed = jnp.zeros_like(raw_noise)
    for offset in range(5):
        smoothed = smoothed + tap_weights[offset] * jnp.roll(raw_noise, offset - 2, axis=-1)
    return smoothed / math.sqrt(19.0)


def draw_data(key, part):
    split_keys = jax.random.split(jax.random.fold_in(key, 101), 9)
    base_key, gain_key, wobble_key, level_key, noise_key = (split_keys[0], split_keys[1], split_keys[2], split_keys[3], split_keys[4])
    whole_key, phase_key, trend_key, rough_key = (split_keys[5], split_keys[6], split_keys[7], split_keys[8])
    full_shape = (SURVEYS, NXTOT, TY, NT)
    raw_base = jax.random.normal(base_key, (1, NXTOT, TY, NT), jnp.float32)
    noise_part = jax.random.normal(noise_key, full_shape, jnp.float32)
    common = 1.5 * time_smooth(raw_base)
    delayed_list = []
    for delay_steps in range(3):
        delayed_list.append(jnp.roll(common[0], delay_steps, axis=-1))
    delayed = jnp.stack(delayed_list)
    whole_delay = jax.random.randint(whole_key, (SURVEYS,), 0, 2)
    phases = jax.random.uniform(phase_key, (4, SURVEYS, 1, 1, 1), jnp.float32, -math.pi, math.pi)
    inline_pos = jnp.arange(NXTOT, dtype=jnp.float32)[None, :, None, None] / NXTOT
    cross_pos = jnp.arange(TY, dtype=jnp.float32)[None, None, :, None] / TY
    rough_part = jax.random.uniform(rough_key, (SURVEYS, NXTOT, TY, 1), jnp.float32, -1.0, 1.0)
    fraction = 0.5 + 0.2 * jnp.sin(2.0 * math.pi * inline_pos + phases[0]) + 0.15 * jnp.sin(2.0 * math.pi * cross_pos + phases[1]) + 0.1 * rough_part
    earlier = jnp.take(delayed, whole_delay, axis=0)
    later = jnp.take(delayed, whole_delay + 1, axis=0)
    shifted = earlier + fraction * (later - earlier)
    trend = jax.random.uniform(trend_key, (SURVEYS, 1, 1, 1), jnp.float32, -0.5, 0.5) + 0.15 * jnp.sin(2.0 * math.pi * inline_pos + phases[2]) + 0.1 * jnp.sin(2.0 * math.pi * cross_pos + phases[3])
    time_pos = (jnp.arange(NT, dtype=jnp.float32) - (NT - 1) / 2.0) / (NT / 2.0)
    group_gain = jnp.exp(0.4 * jax.random.normal(gain_key, (SURVEYS, 1, 1, 1), jnp.float32))
    wobble = 1.0 + 0.3 * jax.random.uniform(wobble_key, (SURVEYS, NXTOT, TY, 1), jnp.float32, -1.0, 1.0)
    noise_level = jnp.exp(jax.random.uniform(level_key, (SURVEYS, 1, 1, 1), jnp.float32, math.log(0.15), 0.0))
    amplitude = group_gain * wobble * jnp.exp(trend * time_pos)
    values = amplitude * shifted + noise_level * noise_part
    return jnp.clip(values, -12.0, 12.0).astype(jnp.bfloat16)


def draw_correlation_count(key, part):
    draw_key, tile_key, group_key = jax.random.split(jax.random.fold_in(key, 202), 3)
    counts = jax.random.randint(draw_key, (SURVEYS, TILES, SURVEYS), 0, CAP + 1)
    source_ids = jnp.arange(SURVEYS, dtype=jnp.int32)[:, None, None]
    tile_ids = jnp.arange(TILES, dtype=jnp.int32)[None, :, None]
    dest_ids = jnp.arange(SURVEYS, dtype=jnp.int32)[None, None, :]
    busy_tile = jax.random.randint(tile_key, (), 0, TILES)
    busy_group = jax.random.randint(group_key, (), 0, SURVEYS)
    counts = jnp.where((tile_ids == busy_tile) & (dest_ids == busy_group), CAP, counts)
    neighbour = (dest_ids + 1) % SURVEYS
    counts = jnp.where(source_ids == neighbour, jnp.maximum(counts, 1), counts)
    counts = jnp.where(source_ids == dest_ids, 0, counts)
    return counts.astype(jnp.int32)


def draw_correlation_index(key, part):
    start_key, tile_key = jax.random.split(jax.random.fold_in(key, 303))
    trace_total = TX * TY
    starts = jax.random.randint(start_key, (SURVEYS, TILES, SURVEYS, 1), 0, trace_total - CAP + 1)
    edge_tile = jax.random.randint(tile_key, (), 0, TILES)
    tile_ids = jnp.arange(TILES, dtype=jnp.int32)[None, :, None, None]
    source_ids = jnp.arange(SURVEYS, dtype=jnp.int32)[:, None, None, None]
    starts = jnp.where((tile_ids == edge_tile) & (source_ids == 0), trace_total - CAP, starts)
    starts = jnp.where((tile_ids == edge_tile) & (source_ids == SURVEYS - 1), 0, starts)
    slot_ids = jnp.arange(CAP, dtype=jnp.int32)[None, None, None, :]
    return (starts + slot_ids).astype(jnp.int32)


def setup_inputs(seed: int = 0) -> dict:
    keys = jax.random.split(jax.random.key(seed), 5)
    return {
        "data": draw_data(jax.random.fold_in(keys[4], 71), 0),
        "correlation_index": draw_correlation_index(jax.random.fold_in(keys[4], 71), 0),
        "correlation_count": draw_correlation_count(jax.random.fold_in(keys[4], 71), 0),
        "smoothing": jnp.clip(jnp.exp(jax.random.uniform(keys[3], (3,), jnp.float32, math.log(0.5), math.log(4.0))), 0.5, 4.0),
    }


damping = 0.05
sim_eps = 1e-5


def time_axis(samples):
    return (jnp.arange(samples, dtype=jnp.float32) - (samples - 1) / 2.0) / (samples / 2.0)


def time_slope(trace_rows):
    padded = jnp.pad(trace_rows, [(0, 0)] * (trace_rows.ndim - 1) + [(1, 1)])
    return 0.5 * (padded[..., 2:] - padded[..., :-2])


def corrected(raw_rows, time_shift, log_gain, gain_trend):
    values = raw_rows.astype(jnp.float32)
    time_pos = time_axis(raw_rows.shape[-1])
    amplitude = jnp.exp(log_gain[..., None] + gain_trend[..., None] * time_pos)
    return (amplitude * (values + time_shift[..., None] * time_slope(values))).astype(jnp.bfloat16)


def pair_terms(own_rows, partner_rows, live_mask):
    own_vals = own_rows.astype(jnp.float32)
    partner_vals = partner_rows.astype(jnp.float32)
    time_pos = time_axis(own_vals.shape[-1])
    residual = partner_vals - own_vals
    moved = time_slope(own_vals)
    tilted = time_pos * own_vals
    energy = jnp.mean(own_vals * own_vals, axis=-1)
    cross_term = jnp.mean(own_vals * partner_vals, axis=-1)
    other_energy = jnp.mean(partner_vals * partner_vals, axis=-1)
    weight = live_mask * cross_term * cross_term / ((energy + sim_eps) * (other_energy + sim_eps))
    numerator = jnp.stack([jnp.mean(residual * moved, axis=-1), jnp.mean(residual * own_vals, axis=-1),
                           jnp.mean(residual * tilted, axis=-1)])
    denominator = jnp.stack([jnp.mean(moved * moved, axis=-1), energy, jnp.mean(tilted * tilted, axis=-1)])
    return weight * numerator, weight * denominator


def survey_terms(dest_group, current, correlation_index, correlation_count):
    groups = current.shape[0]
    index_dest = lax.dynamic_index_in_dim(correlation_index, dest_group, axis=2, keepdims=False)
    count_dest = lax.dynamic_index_in_dim(correlation_count, dest_group, axis=2, keepdims=False)
    group_ids = jnp.arange(groups, dtype=jnp.int32)[:, None, None]
    tile_ids = jnp.arange(N_TILE, dtype=jnp.int32)[None, :, None]
    partner_rows = current[group_ids, tile_ids, index_dest]
    own_all = lax.dynamic_index_in_dim(current, dest_group, axis=0, keepdims=False)
    own_rows = own_all[tile_ids, index_dest]
    slot_ids = jnp.arange(CAP, dtype=jnp.int32)
    live_mask = (slot_ids[None, None, :] < count_dest[..., None]).astype(jnp.float32)
    numerator, denominator = pair_terms(own_rows, partner_rows, live_mask)
    empty_sum = jnp.zeros((3, N_TILE, TX * TY), jnp.float32)
    target = empty_sum.at[:, tile_ids, index_dest].add(numerator)
    weights = empty_sum.at[:, tile_ids, index_dest].add(denominator)
    return target.reshape(3, NXTOT, TY), weights.reshape(3, NXTOT, TY)


def smooth_apply(field, weights, smoothing):
    padded = jnp.pad(field, ((0, 0), (0, 0), (1, 1), (1, 1)))
    beside = padded[:, :, 2:, 1:-1] + padded[:, :, :-2, 1:-1] + padded[:, :, 1:-1, 2:] + padded[:, :, 1:-1, :-2]
    strength = smoothing[None, :, None, None]
    return (weights + damping + 4.0 * strength) * field - strength * beside


def conjugate(target, weights, smoothing):
    solution = jnp.zeros_like(target)
    residual = target
    direction = target
    norm_now = jnp.sum(residual * residual, axis=(2, 3))
    for iteration in range(CG_ITERS):
        image = smooth_apply(direction, weights, smoothing)
        alpha = norm_now / jnp.sum(direction * image, axis=(2, 3))
        solution = solution + alpha[:, :, None, None] * direction
        residual = residual - alpha[:, :, None, None] * image
        norm_next = jnp.sum(residual * residual, axis=(2, 3))
        direction = residual + (norm_next / norm_now)[:, :, None, None] * direction
        norm_now = norm_next
    return solution


def reference(data, correlation_index, correlation_count, smoothing):
    groups = data.shape[0]
    stacked = data.reshape(groups, N_TILE, TX * TY, NT)
    fields = jnp.zeros((groups, 3, NXTOT, TY), jnp.float32)
    for outer_round in range(ROUNDS):
        flat_fields = fields.reshape(groups, 3, N_TILE, TX * TY)
        current = corrected(stacked, flat_fields[:, 0], flat_fields[:, 1], flat_fields[:, 2])

        def per_group(dest_group):
            return survey_terms(dest_group, current, correlation_index, correlation_count)

        target, weights = lax.map(per_group, jnp.arange(groups, dtype=jnp.int32))
        fields = fields + conjugate(target, weights, smoothing)
    flat_fields = fields.reshape(groups, 3, N_TILE, TX * TY)
    volume = corrected(stacked, flat_fields[:, 0], flat_fields[:, 1], flat_fields[:, 2])
    return fields, volume.reshape(groups, NXTOT, TY, NT)
```

```python
import functools

import jax
import jax.numpy as jnp
from jax import lax
from jax.experimental import pallas as pl
from jax.experimental.pallas import tpu as pltpu
from jax.sharding import PartitionSpec as P

ROUNDS = 2
DAMPING = 0.05
SIM_EPS = 1e-05
CG_ITERS = 3
CHUNK = 32
LANES = 128
F32 = jnp.float32
BF16 = jnp.bfloat16


def slope_of(v):
    n = v.shape[0]
    row = lax.broadcasted_iota(jnp.int32, v.shape, 0)
    after = jnp.where(row == n - 1, 0.0, pltpu.roll(v, n - 1, 0))
    before = jnp.where(row == 0, 0.0, pltpu.roll(v, 1, 0))
    return 0.5 * (after - before)


def time_rows(start, length, samples):
    row = lax.broadcasted_iota(jnp.int32, (length, LANES), 0) + start
    return (row.astype(F32) - (samples - 1) / 2.0) / (samples / 2.0)


def fold(a):
    return jnp.sum(a.reshape(a.shape[0] // 8, 8, a.shape[1]), axis=0)


def kernel(
    survey_n, tile_n, data_hbm, index_hbm, count_hbm, strength_hbm, fields_ref,
    data, send_index, recv_index, count_ref, strength_ref, raw, raw_slope, own, own_slope, stats,
    out_lists, in_lists, list_raw, list_slope,
    edge_out, edge_low, edge_high, moment_out, moment_in, field_rows, field_out, field_in,
    load_sem, list_send, list_recv, edge_send, edge_recv, moment_send, moment_recv, field_send, field_recv,
):
    rows_x, rows_y, samples = data.shape
    me = lax.axis_index("survey")
    tile = lax.axis_index("tile")
    peers = survey_n - 1
    others = tile_n - 1
    lane = lax.broadcasted_iota(jnp.int32, (8, LANES), 1)
    sub = lax.broadcasted_iota(jnp.int32, (8, LANES), 0)
    lane1 = lax.broadcasted_iota(jnp.int32, (1, LANES), 1)

    def offset(j):
        half = (j + 1) // 2
        return jnp.where(j % 2 == 0, half + 1, survey_n - half)

    def receiver(j):
        return lax.rem(me + offset(j), survey_n)

    def sender(j):
        return lax.rem(me + survey_n - offset(j), survey_n)

    loads = [
        pltpu.make_async_copy(index_hbm.at[me, 0], send_index, load_sem.at[0]),
        pltpu.make_async_copy(data_hbm.at[0], data, load_sem.at[1]),
        pltpu.make_async_copy(index_hbm.at[:, 0, me], recv_index, load_sem.at[2]),
        pltpu.make_async_copy(count_hbm, count_ref, load_sem.at[3]),
        pltpu.make_async_copy(strength_hbm, strength_ref, load_sem.at[4]),
    ]
    for load in loads:
        load.start()
    barrier = pltpu.get_barrier_semaphore()

    def greet_survey(i, c):
        pl.semaphore_signal(barrier, inc=1, device_id={"survey": lax.rem(me + i, survey_n)},
                            device_id_type=pl.DeviceIdType.MESH)
        return c

    def greet_tile(i, c):
        pl.semaphore_signal(barrier, inc=1, device_id={"tile": lax.rem(tile + i, tile_n)},
                            device_id_type=pl.DeviceIdType.MESH)
        return c

    lax.fori_loop(1, survey_n, greet_survey, 0)
    lax.fori_loop(1, tile_n, greet_tile, 0)
    loads[0].wait()
    loads[1].wait()

    def list_copy(j):
        return pltpu.make_async_remote_copy(
            src_ref=out_lists.at[j], dst_ref=in_lists.at[j], send_sem=list_send.at[j],
            recv_sem=list_recv.at[j], device_id={"survey": receiver(j)},
            device_id_type=pl.DeviceIdType.MESH)

    def build_list(j):
        start = send_index[receiver(j), 0]
        x0 = start // LANES
        y0 = start % LANES
        x1 = jnp.minimum(x0 + 1, rows_x - 1)
        for y in range(0, rows_y, CHUNK):
            place = lax.broadcasted_iota(jnp.int32, (CHUNK, samples), 0) + y
            first = place.astype(F32).astype(BF16) >= jnp.full((CHUNK, samples), y0, jnp.int32).astype(F32).astype(BF16)
            out_lists[j, y:y + CHUNK, :] = jnp.where(first, data[x0, y:y + CHUNK, :], data[x1, y:y + CHUNK, :])

    build_list(0)
    pl.semaphore_wait(barrier, peers + others)
    list_copy(0).start()

    def send_list(j, c):
        build_list(j)
        list_copy(j).start()
        return c

    lax.fori_loop(1, peers, send_list, 0)
    for load in loads[2:]:
        load.wait()

    def row_stats(x, slopes, values):
        sums = [jnp.zeros((8, LANES), F32) for _ in range(5)]
        for t in range(0, samples, CHUNK):
            u = values[x, t:t + CHUNK, :].astype(F32)
            a = slopes[x, t:t + CHUNK, :]
            w = u * time_rows(t, CHUNK, samples)
            for k, (p, q) in enumerate(((u, u), (a, a), (w, w), (u, a), (u, w))):
                sums[k] = sums[k] + fold(p * q)
        for k in range(5):
            stats[k, pl.ds(x, 1), :] = jnp.sum(sums[k], axis=0, keepdims=True) * (1.0 / samples)

    def first_own(x, c):
        raw[x] = data[x].T
        raw_slope[x] = slope_of(raw[x].astype(F32))
        row_stats(x, raw_slope, raw)
        return c

    lax.fori_loop(0, rows_x, first_own, 0)

    def later_own(x, c):
        shift = fields_ref[0, 0, pl.ds(x, 1), :]
        log_gain = fields_ref[0, 1, pl.ds(x, 1), :]
        trend = fields_ref[0, 2, pl.ds(x, 1), :]
        for t in range(0, samples, CHUNK):
            amplitude = jnp.exp(log_gain + trend * time_rows(t, CHUNK, samples))
            d = raw[x, t:t + CHUNK, :].astype(F32)
            own[x, t:t + CHUNK, :] = (amplitude * (d + shift * raw_slope[x, t:t + CHUNK, :])).astype(BF16)
        own_slope[x] = slope_of(own[x].astype(F32))
        row_stats(x, own_slope, own)
        return c

    def list_terms(j, carry, values, slopes, partner):
        total, t0, t1, t2 = carry
        source = sender(j)
        start = recv_index[source, 0]
        count = count_ref[source, 0, me]
        x0 = start // LANES
        y0 = start % LANES
        x1 = jnp.minimum(x0 + 1, rows_x - 1)
        y = lax.broadcasted_iota(jnp.int32, (CHUNK, LANES), 1)
        first = y >= y0
        sums = [jnp.zeros((8, LANES), F32) for _ in range(4)]
        for t in range(0, samples, CHUNK):
            v = partner(j, t)
            u = jnp.where(first, values[x0, t:t + CHUNK, :], values[x1, t:t + CHUNK, :]).astype(F32)
            a = jnp.where(first, slopes[x0, t:t + CHUNK, :], slopes[x1, t:t + CHUNK, :])
            uv = u * v
            sums[0] = sums[0] + fold(uv)
            sums[1] = sums[1] + fold(a * v)
            sums[2] = sums[2] + fold(uv * time_rows(t, CHUNK, samples))
            sums[3] = sums[3] + fold(v * v)
        uv, av, wv, vv = [jnp.sum(s, axis=0, keepdims=True) * (1.0 / samples) for s in sums]
        slot = sub * LANES + lane - start
        live = (slot >= 0) & (slot < count)
        uu = stats[0]
        weight = jnp.where(live, (uv * uv) / ((uu + SIM_EPS) * (vv + SIM_EPS)), 0.0)
        return (total + weight, t0 + weight * (av - stats[3]), t1 + weight * (uv - uu),
                t2 + weight * (wv - stats[4]))

    def first_list(j, carry):
        list_copy(j).wait_recv()
        d = in_lists[j].T
        list_raw[j] = d
        return list_terms(j, carry, raw, raw_slope, lambda j, t: list_raw[j, t:t + CHUNK, :].astype(F32))

    def later_partner(j, t):
        shift = field_in[j, 0:1, :]
        log_gain = field_in[j, 1:2, :]
        trend = field_in[j, 2:3, :]
        amplitude = jnp.exp(log_gain + trend * time_rows(t, CHUNK, samples))
        d = list_raw[j, t:t + CHUNK, :].astype(F32)
        return (amplitude * (d + shift * list_slope[j, t:t + CHUNK, :])).astype(BF16).astype(F32)

    def field_copy(j):
        return pltpu.make_async_remote_copy(
            src_ref=field_out.at[j], dst_ref=field_in.at[j], send_sem=field_send.at[j],
            recv_sem=field_recv.at[j], device_id={"survey": receiver(j)},
            device_id_type=pl.DeviceIdType.MESH)

    def later_list(j, carry):
        field_copy(j).wait_recv()
        return list_terms(j, carry, own, own_slope, later_partner)

    def send_fields(i, c):
        j = peers - 1 - i
        start = send_index[receiver(j), 0]
        x0 = start // LANES
        y0 = start % LANES
        x1 = jnp.minimum(x0 + 1, rows_x - 1)
        field_out[j] = jnp.where(lane >= y0, field_rows[x0], field_rows[x1])
        field_copy(j).start()
        return c

    def edge_copy(side, r):
        step = 1 if side == 0 else tile_n - 1
        return pltpu.make_async_remote_copy(
            src_ref=edge_out.at[r], dst_ref=(edge_low if side == 0 else edge_high).at[r],
            send_sem=edge_send.at[r, side], recv_sem=edge_recv.at[r, side],
            device_id={"tile": lax.rem(tile + step, tile_n)}, device_id_type=pl.DeviceIdType.MESH)

    def moment_copy(r, d):
        return pltpu.make_async_remote_copy(
            src_ref=moment_out.at[r], dst_ref=moment_in.at[r, d],
            send_sem=moment_send.at[r], recv_sem=moment_recv.at[r],
            device_id={"tile": lax.rem(tile + d, tile_n)}, device_id_type=pl.DeviceIdType.MESH)

    def moment_all(r):
        return pltpu.make_async_remote_copy(
            src_ref=moment_in.at[r, pl.ds(1, others)], dst_ref=moment_in.at[r, pl.ds(1, others)],
            send_sem=moment_send.at[r], recv_sem=moment_recv.at[r],
            device_id={"tile": lax.rem(tile + 1, tile_n)}, device_id_type=pl.DeviceIdType.MESH)

    def slope_list(j, c):
        list_slope[j] = slope_of(list_raw[j].astype(F32))
        return c

    def solve(r, total, t0, t1, t2):
        for c, t in enumerate((t0, t1, t2)):
            edge_out[r, c] = t
        edge_out[r, 3] = total * stats[1]
        edge_out[r, 4] = total * stats[0]
        edge_out[r, 5] = total * stats[2]
        edge_copy(0, r).start()
        edge_copy(1, r).start()
        if r == 0:
            lax.fori_loop(0, peers, slope_list, 0)
        edge_copy(0, r).wait_recv()
        edge_copy(1, r).wait_recv()

        row = lax.broadcasted_iota(jnp.int32, (24, LANES), 0)
        col = lax.broadcasted_iota(jnp.int32, (24, LANES), 1)
        inside = ((row >= 8) | (tile > 0)) & ((row < 16) | (tile < tile_n - 1))
        state = []
        for c in range(3):
            strength = strength_ref[c]
            b = jnp.where(inside, jnp.concatenate([edge_low[r, c], edge_out[r, c], edge_high[r, c]], axis=0), 0.0)
            w = jnp.where(inside, jnp.concatenate(
                [edge_low[r, 3 + c], edge_out[r, 3 + c], edge_high[r, 3 + c]], axis=0), 0.0)
            bound = jnp.max(jnp.max(w, axis=0, keepdims=True), axis=1, keepdims=True) + (DAMPING + 8.0 * strength)
            scale = 1.0 / bound
            diagonal = (w + DAMPING + 4.0 * strength) * scale
            state.append([b, b, None, bound, diagonal, strength * scale])

        def apply(y, diagonal, off):
            up = pltpu.roll(y, 1, 0)
            down = pltpu.roll(y, 23, 0)
            left = jnp.where(col == 0, 0.0, pltpu.roll(y, 1, 1))
            right = jnp.where(col == LANES - 1, 0.0, pltpu.roll(y, LANES - 1, 1))
            return jnp.where(inside, diagonal * y - off * (up + down + left + right), 0.0)

        power = lane1 % 8

        def powers(q):
            return jnp.where(power == 1, q, 1.0) * jnp.where(power == 2, q * q, 1.0)

        for step in range(CG_ITERS):
            slot = r * CG_ITERS + step
            message = jnp.where(lane1 >= 64, 1.0, 0.0).astype(F32)
            images = []
            for c in range(3):
                residual, direction, update, bound, diagonal, off = state[c]
                image = apply(direction, diagonal, off)
                images.append(image)
                p0, p1, q1 = residual[8:16], direction[8:16], image[8:16]
                block = jnp.zeros((8, LANES), F32)
                for k, (p, q) in enumerate(((p0, p0), (p1, q1), (q1, q1))):
                    block = jnp.where(sub == k, jnp.sum(p * q, axis=0, keepdims=True), block)
                sums = jnp.sum(block, axis=1, keepdims=True)
                message = message + jnp.sum(jnp.where(lane == 8 * c + sub, sums, 0.0), axis=0, keepdims=True)
                message = jnp.where((lane1 >= 64 + 8 * c) & (lane1 < 72 + 8 * c), bound, message)
            moment_out[slot] = message
            moment_in[slot, 0] = message

            def send_moments(i, c):
                half = (i + 1) // 2
                moment_copy(slot, tile_n // 2 + jnp.where(i % 2 == 0, half, -half)).start()
                return c

            lax.fori_loop(0, others, send_moments, 0)
            moment_all(slot).wait_recv()
            rows = [moment_in[slot, d] for d in range(tile_n)]
            bounds = [pltpu.roll(m, 64, 1) for m in rows]
            top = functools.reduce(jnp.maximum, bounds)
            inverse = 1.0 / top
            m0 = jnp.zeros((1, LANES), F32)
            for d in range(tile_n):
                m0 = m0 + rows[d] * powers(bounds[d] * inverse)
            m1, m2 = [pltpu.roll(m0, LANES - k, 1) for k in (1, 2)]
            alpha = m0 / m1
            beta = jnp.maximum(alpha * alpha * m2 - m0, 0.0) / m0
            along = alpha * inverse
            back = alpha * inverse * bounds[0]
            for c in range(3):
                k1, k2, k3 = [jnp.sum(jnp.where(lane1 == 8 * c, z, 0.0), axis=1, keepdims=True)
                              for z in (along, back, beta)]
                residual, direction, update = state[c][:3]
                part = k1 * direction[8:16]
                state[c][2] = part if step == 0 else update + part
                state[c][0] = residual - k2 * images[c]
                state[c][1] = state[c][0] + k3 * direction
        for c in range(3):
            fields_ref[0, c] = state[c][2] if r == 0 else fields_ref[0, c] + state[c][2]

    zero = jnp.zeros((8, LANES), F32)
    carry = lax.fori_loop(0, peers, first_list, (zero,) * 4)
    solve(0, *carry)
    for x in range(rows_x):
        for c in range(3):
            field_rows[x, c:c + 1, :] = fields_ref[0, c, x:x + 1, :]
        field_rows[x, 3:8, :] = jnp.zeros((5, LANES), F32)
    lax.fori_loop(0, peers, send_fields, 0)
    lax.fori_loop(0, rows_x, later_own, 0)
    carry = lax.fori_loop(0, peers, later_list, (zero,) * 4)
    solve(1, *carry)

    def drain(j, c):
        list_copy(j).wait_send()
        field_copy(j).wait_send()
        return c

    lax.fori_loop(0, peers, drain, 0)
    for r in range(ROUNDS):
        edge_copy(0, r).wait_send()
        edge_copy(1, r).wait_send()
        for step in range(CG_ITERS):
            moment_all(r * CG_ITERS + step).wait_send()


def correct_kernel(data_hbm, fields_hbm, fields_out, volume_hbm, data, fields, volume, load_sem, store_sem):
    rows_x, rows_y, samples = data.shape
    parts = load_sem.shape[0] - 1
    rows = rows_x // parts
    lane = lax.broadcasted_iota(jnp.int32, (rows_y, samples), 1)
    time_pos = (lane.astype(F32) - (samples - 1) / 2.0) / (samples / 2.0)
    field_load = pltpu.make_async_copy(fields_hbm, fields, load_sem.at[parts])
    field_load.start()

    def load(k):
        part = pl.ds(k * rows, rows)
        return pltpu.make_async_copy(data_hbm.at[0, part], data.at[part], load_sem.at[k])

    def store(k):
        part = pl.ds(k * rows, rows)
        return pltpu.make_async_copy(volume.at[part], volume_hbm.at[0, part], store_sem.at[k])

    for k in range(parts):
        load(k).start()
    field_load.wait()
    field_store = pltpu.make_async_copy(fields, fields_out, store_sem.at[parts])
    field_store.start()
    columns = [fields[0, c].T for c in range(3)]
    for k in range(parts):
        load(k).wait()
        for x in range(k * rows, (k + 1) * rows):
            shift, log_gain, trend = [column[:, x:x + 1] for column in columns]
            d = data[x].astype(F32)
            after = jnp.where(lane == samples - 1, 0.0, pltpu.roll(d, samples - 1, 1))
            before = jnp.where(lane == 0, 0.0, pltpu.roll(d, 1, 1))
            amplitude = jnp.exp(log_gain + trend * time_pos)
            volume[x] = (amplitude * (d + shift * (0.5 * (after - before)))).astype(BF16)
        store(k).start()
    for k in range(parts):
        store(k).wait()
    field_store.wait()


def correct(data, fields):
    rows_x, rows_y, samples = data.shape[1:]
    parts = 4
    block = pltpu.VMEM((rows_x, rows_y, samples), BF16)
    return pl.pallas_call(
        correct_kernel,
        out_shape=(jax.ShapeDtypeStruct(fields.shape, F32), jax.ShapeDtypeStruct(data.shape, BF16)),
        in_specs=[pl.BlockSpec(memory_space=pl.ANY)] * 2,
        out_specs=[pl.BlockSpec(memory_space=pl.ANY)] * 2,
        scratch_shapes=[block, pltpu.VMEM(fields.shape, F32), block,
                        pltpu.SemaphoreType.DMA((parts + 1,)), pltpu.SemaphoreType.DMA((parts + 1,))],
        compiler_params=pltpu.CompilerParams(vmem_limit_bytes=60 * 1024 * 1024),
    )(data, fields)


def local(data, correlation_index, correlation_count, smoothing):
    survey_n = lax.axis_size("survey")
    tile_n = lax.axis_size("tile")
    rows_x, rows_y, samples = data.shape[1:]
    peers = survey_n - 1
    block = (samples, LANES)
    turned = (LANES, samples)
    dma = pltpu.SemaphoreType.DMA
    fields = pl.pallas_call(
        functools.partial(kernel, survey_n, tile_n),
        out_shape=jax.ShapeDtypeStruct((1, 3, rows_x, rows_y), F32),
        in_specs=[pl.BlockSpec(memory_space=pl.ANY)] * 4,
        out_specs=pl.BlockSpec(memory_space=pltpu.VMEM),
        scratch_shapes=[
            pltpu.VMEM((rows_x,) + turned, BF16),
            pltpu.SMEM((survey_n, correlation_index.shape[3]), jnp.int32),
            pltpu.SMEM((survey_n, correlation_index.shape[3]), jnp.int32),
            pltpu.SMEM(correlation_count.shape, jnp.int32),
            pltpu.SMEM(smoothing.shape, F32),
            pltpu.VMEM((rows_x,) + block, BF16),
            pltpu.VMEM((rows_x,) + block, F32),
            pltpu.VMEM((rows_x,) + block, BF16),
            pltpu.VMEM((rows_x,) + block, F32),
            pltpu.VMEM((5, rows_x, LANES), F32),
            pltpu.VMEM((peers,) + turned, BF16),
            pltpu.VMEM((peers,) + turned, BF16),
            pltpu.VMEM((peers,) + block, BF16),
            pltpu.VMEM((peers,) + block, F32),
            pltpu.VMEM((ROUNDS, 6, rows_x, LANES), F32),
            pltpu.VMEM((ROUNDS, 6, rows_x, LANES), F32),
            pltpu.VMEM((ROUNDS, 6, rows_x, LANES), F32),
            pltpu.VMEM((ROUNDS * CG_ITERS, 1, LANES), F32),
            pltpu.VMEM((ROUNDS * CG_ITERS, tile_n, 1, LANES), F32),
            pltpu.VMEM((rows_x, 8, LANES), F32),
            pltpu.VMEM((peers, 8, LANES), F32),
            pltpu.VMEM((peers, 8, LANES), F32),
            dma((5,)),
            dma((peers,)), dma((peers,)),
            dma((ROUNDS, 2)), dma((ROUNDS, 2)),
            dma((ROUNDS * CG_ITERS,)), dma((ROUNDS * CG_ITERS,)),
            dma((peers,)), dma((peers,)),
        ],
        compiler_params=pltpu.CompilerParams(
            collective_id=0, has_side_effects=True, vmem_limit_bytes=60 * 1024 * 1024),
    )(data, correlation_index, correlation_count, smoothing)
    return correct(data, fields)


def solution(mesh):
    placed = (
        P("survey", "tile", None, None),
        P(None, "tile", None, None),
        P(None, "tile", None),
        P(),
    )
    return jax.shard_map(
        local,
        mesh=mesh,
        in_specs=placed,
        out_specs=(P("survey", None, "tile", None), P("survey", "tile", None, None)),
        check_vma=False,
    )
```

```python
import functools

import jax
import jax.numpy as jnp
from jax import lax
from jax.experimental import pallas as pl
from jax.experimental.pallas import tpu as pltpu
from jax.sharding import PartitionSpec as P

ROUNDS = 2
DAMPING = 0.05
SIM_EPS = 1e-05
SUMS = 2
PIVOT = 3e-07
CHUNK = 32
LANES = 128
F32 = jnp.float32
BF16 = jnp.bfloat16


def slope_of(v):
    n = v.shape[0]
    row = lax.broadcasted_iota(jnp.int32, v.shape, 0)
    after = jnp.where(row == n - 1, 0.0, pltpu.roll(v, n - 1, 0))
    before = jnp.where(row == 0, 0.0, pltpu.roll(v, 1, 0))
    return 0.5 * (after - before)


def time_rows(start, length, samples):
    row = lax.broadcasted_iota(jnp.int32, (length, LANES), 0) + start
    return (row.astype(F32) - (samples - 1) / 2.0) / (samples / 2.0)


def fold(a):
    return jnp.sum(a.reshape(a.shape[0] // 8, 8, a.shape[1]), axis=0)


def kernel(
    survey_n, tile_n, data_hbm, index_hbm, count_hbm, strength_hbm, fields_ref,
    data, send_index, recv_index, count_ref, strength_ref, raw, raw_slope, own, own_slope, stats,
    out_lists, in_lists, list_raw, list_slope,
    edge_out, edge_low, edge_high, moment_out, moment_in, field_rows, field_out, field_in,
    load_sem, list_send, list_recv, edge_send, edge_recv, moment_send, moment_recv, field_send, field_recv,
):
    rows_x, rows_y, samples = data.shape
    me = lax.axis_index("survey")
    tile = lax.axis_index("tile")
    peers = survey_n - 1
    others = tile_n - 1
    lane = lax.broadcasted_iota(jnp.int32, (8, LANES), 1)
    sub = lax.broadcasted_iota(jnp.int32, (8, LANES), 0)
    lane1 = lax.broadcasted_iota(jnp.int32, (1, LANES), 1)

    def offset(j):
        half = (j + 1) // 2
        return jnp.where(j % 2 == 0, half + 1, survey_n - half)

    def receiver(j):
        return lax.rem(me + offset(j), survey_n)

    def sender(j):
        return lax.rem(me + survey_n - offset(j), survey_n)

    loads = [
        pltpu.make_async_copy(index_hbm.at[me, 0], send_index, load_sem.at[0]),
        pltpu.make_async_copy(data_hbm.at[0], data, load_sem.at[1]),
        pltpu.make_async_copy(index_hbm.at[:, 0, me], recv_index, load_sem.at[2]),
        pltpu.make_async_copy(count_hbm, count_ref, load_sem.at[3]),
        pltpu.make_async_copy(strength_hbm, strength_ref, load_sem.at[4]),
    ]
    for load in loads:
        load.start()
    barrier = pltpu.get_barrier_semaphore()

    def greet_survey(i, c):
        pl.semaphore_signal(barrier, inc=1, device_id={"survey": lax.rem(me + i, survey_n)},
                            device_id_type=pl.DeviceIdType.MESH)
        return c

    def greet_tile(i, c):
        pl.semaphore_signal(barrier, inc=1, device_id={"tile": lax.rem(tile + i, tile_n)},
                            device_id_type=pl.DeviceIdType.MESH)
        return c

    lax.fori_loop(1, survey_n, greet_survey, 0)
    lax.fori_loop(1, tile_n, greet_tile, 0)
    loads[0].wait()
    loads[1].wait()

    def list_copy(j):
        return pltpu.make_async_remote_copy(
            src_ref=out_lists.at[j], dst_ref=in_lists.at[j], send_sem=list_send.at[j],
            recv_sem=list_recv.at[j], device_id={"survey": receiver(j)},
            device_id_type=pl.DeviceIdType.MESH)

    def build_list(j):
        start = send_index[receiver(j), 0]
        x0 = start // LANES
        y0 = start % LANES
        x1 = jnp.minimum(x0 + 1, rows_x - 1)
        for y in range(0, rows_y, CHUNK):
            place = lax.broadcasted_iota(jnp.int32, (CHUNK, samples), 0) + y
            first = place.astype(F32).astype(BF16) >= jnp.full((CHUNK, samples), y0, jnp.int32).astype(F32).astype(BF16)
            out_lists[j, y:y + CHUNK, :] = jnp.where(first, data[x0, y:y + CHUNK, :], data[x1, y:y + CHUNK, :])

    build_list(0)
    pl.semaphore_wait(barrier, peers + others)
    list_copy(0).start()

    def send_list(j, c):
        build_list(j)
        list_copy(j).start()
        return c

    lax.fori_loop(1, peers, send_list, 0)
    for load in loads[2:]:
        load.wait()

    def row_stats(x, slopes, values):
        sums = [jnp.zeros((8, LANES), F32) for _ in range(5)]
        for t in range(0, samples, CHUNK):
            u = values[x, t:t + CHUNK, :].astype(F32)
            a = slopes[x, t:t + CHUNK, :]
            w = u * time_rows(t, CHUNK, samples)
            for k, (p, q) in enumerate(((u, u), (a, a), (w, w), (u, a), (u, w))):
                sums[k] = sums[k] + fold(p * q)
        for k in range(5):
            stats[k, pl.ds(x, 1), :] = jnp.sum(sums[k], axis=0, keepdims=True) * (1.0 / samples)

    def first_own(x, c):
        raw[x] = data[x].T
        raw_slope[x] = slope_of(raw[x].astype(F32))
        row_stats(x, raw_slope, raw)
        return c

    lax.fori_loop(0, rows_x, first_own, 0)

    def later_own(x, c):
        shift = fields_ref[0, 0, pl.ds(x, 1), :]
        log_gain = fields_ref[0, 1, pl.ds(x, 1), :]
        trend = fields_ref[0, 2, pl.ds(x, 1), :]
        for t in range(0, samples, CHUNK):
            amplitude = jnp.exp(log_gain + trend * time_rows(t, CHUNK, samples))
            d = raw[x, t:t + CHUNK, :].astype(F32)
            own[x, t:t + CHUNK, :] = (amplitude * (d + shift * raw_slope[x, t:t + CHUNK, :])).astype(BF16)
        own_slope[x] = slope_of(own[x].astype(F32))
        row_stats(x, own_slope, own)
        return c

    def list_terms(j, carry, values, slopes, partner):
        total, t0, t1, t2 = carry
        source = sender(j)
        start = recv_index[source, 0]
        count = count_ref[source, 0, me]
        x0 = start // LANES
        y0 = start % LANES
        x1 = jnp.minimum(x0 + 1, rows_x - 1)
        y = lax.broadcasted_iota(jnp.int32, (CHUNK, LANES), 1)
        first = y >= y0
        sums = [jnp.zeros((8, LANES), F32) for _ in range(4)]
        for t in range(0, samples, CHUNK):
            v = partner(j, t)
            u = jnp.where(first, values[x0, t:t + CHUNK, :], values[x1, t:t + CHUNK, :]).astype(F32)
            a = jnp.where(first, slopes[x0, t:t + CHUNK, :], slopes[x1, t:t + CHUNK, :])
            uv = u * v
            sums[0] = sums[0] + fold(uv)
            sums[1] = sums[1] + fold(a * v)
            sums[2] = sums[2] + fold(uv * time_rows(t, CHUNK, samples))
            sums[3] = sums[3] + fold(v * v)
        uv, av, wv, vv = [jnp.sum(s, axis=0, keepdims=True) * (1.0 / samples) for s in sums]
        slot = sub * LANES + lane - start
        live = (slot >= 0) & (slot < count)
        uu = stats[0]
        weight = jnp.where(live, (uv * uv) / ((uu + SIM_EPS) * (vv + SIM_EPS)), 0.0)
        return (total + weight, t0 + weight * (av - stats[3]), t1 + weight * (uv - uu),
                t2 + weight * (wv - stats[4]))

    def first_list(j, carry):
        list_copy(j).wait_recv()
        d = in_lists[j].T
        list_raw[j] = d
        return list_terms(j, carry, raw, raw_slope, lambda j, t: list_raw[j, t:t + CHUNK, :].astype(F32))

    def later_partner(j, t):
        shift = field_in[j, 0:1, :]
        log_gain = field_in[j, 1:2, :]
        trend = field_in[j, 2:3, :]
        amplitude = jnp.exp(log_gain + trend * time_rows(t, CHUNK, samples))
        d = list_raw[j, t:t + CHUNK, :].astype(F32)
        return (amplitude * (d + shift * list_slope[j, t:t + CHUNK, :])).astype(BF16).astype(F32)

    def field_copy(j):
        return pltpu.make_async_remote_copy(
            src_ref=field_out.at[j], dst_ref=field_in.at[j], send_sem=field_send.at[j],
            recv_sem=field_recv.at[j], device_id={"survey": receiver(j)},
            device_id_type=pl.DeviceIdType.MESH)

    def later_list(j, carry):
        field_copy(j).wait_recv()
        return list_terms(j, carry, own, own_slope, later_partner)

    def send_fields(i, c):
        j = peers - 1 - i
        start = send_index[receiver(j), 0]
        x0 = start // LANES
        y0 = start % LANES
        x1 = jnp.minimum(x0 + 1, rows_x - 1)
        field_out[j] = jnp.where(lane >= y0, field_rows[x0], field_rows[x1])
        field_copy(j).start()
        return c

    def edge_copy(side, r):
        step = 1 if side == 0 else tile_n - 1
        return pltpu.make_async_remote_copy(
            src_ref=edge_out.at[r], dst_ref=(edge_low if side == 0 else edge_high).at[r],
            send_sem=edge_send.at[r, side], recv_sem=edge_recv.at[r, side],
            device_id={"tile": lax.rem(tile + step, tile_n)}, device_id_type=pl.DeviceIdType.MESH)

    def moment_copy(r, d):
        return pltpu.make_async_remote_copy(
            src_ref=moment_out.at[r], dst_ref=moment_in.at[r, d],
            send_sem=moment_send.at[r], recv_sem=moment_recv.at[r],
            device_id={"tile": lax.rem(tile + d, tile_n)}, device_id_type=pl.DeviceIdType.MESH)

    def moment_all(r):
        return pltpu.make_async_remote_copy(
            src_ref=moment_in.at[r, pl.ds(1, others)], dst_ref=moment_in.at[r, pl.ds(1, others)],
            send_sem=moment_send.at[r], recv_sem=moment_recv.at[r],
            device_id={"tile": lax.rem(tile + 1, tile_n)}, device_id_type=pl.DeviceIdType.MESH)

    def slope_list(j, c):
        list_slope[j] = slope_of(list_raw[j].astype(F32))
        return c

    def solve(r, total, t0, t1, t2):
        for c, t in enumerate((t0, t1, t2)):
            edge_out[r, c] = t
        edge_out[r, 3] = total * stats[1]
        edge_out[r, 4] = total * stats[0]
        edge_out[r, 5] = total * stats[2]
        edge_copy(0, r).start()
        edge_copy(1, r).start()
        if r == 0:
            lax.fori_loop(0, peers, slope_list, 0)
        edge_copy(0, r).wait_recv()
        edge_copy(1, r).wait_recv()

        row = lax.broadcasted_iota(jnp.int32, (24, LANES), 0)
        col = lax.broadcasted_iota(jnp.int32, (24, LANES), 1)
        inside = ((row >= 8) | (tile > 0)) & ((row < 16) | (tile < tile_n - 1))
        state = []
        for c in range(3):
            strength = strength_ref[c]
            b = jnp.where(inside, jnp.concatenate([edge_low[r, c], edge_out[r, c], edge_high[r, c]], axis=0), 0.0)
            w = jnp.where(inside, jnp.concatenate(
                [edge_low[r, 3 + c], edge_out[r, 3 + c], edge_high[r, 3 + c]], axis=0), 0.0)
            bound = jnp.max(jnp.max(w, axis=0, keepdims=True), axis=1, keepdims=True) + (DAMPING + 8.0 * strength)
            scale = 1.0 / bound
            diagonal = (w + DAMPING + 4.0 * strength) * scale
            state.append([b, b, None, bound, diagonal, strength * scale])

        def apply(y, diagonal, off):
            up = pltpu.roll(y, 1, 0)
            down = pltpu.roll(y, 23, 0)
            left = jnp.where(col == 0, 0.0, pltpu.roll(y, 1, 1))
            right = jnp.where(col == LANES - 1, 0.0, pltpu.roll(y, LANES - 1, 1))
            return jnp.where(inside, diagonal * y - off * (up + down + left + right), 0.0)

        power = lane1 % 8

        def powers(q):
            once = (power == 1) | (power == 3) | (power == 5)
            twice = (power == 2) | (power == 4) | (power == 5)
            return jnp.where(once, q, 1.0) * jnp.where(twice, q * q, 1.0)

        for step in range(SUMS):
            slot = r * SUMS + step
            message = jnp.where(lane1 >= 64, 1.0, 0.0).astype(F32)
            images = []
            for c in range(3):
                residual, direction, update, bound, diagonal, off = state[c]
                image = apply(direction, diagonal, off)
                images.append(image)
                p0, p1, q1 = residual[8:16], direction[8:16], image[8:16]
                block = jnp.zeros((8, LANES), F32)
                pairs = [(p0, p0), (p1, q1), (q1, q1)]
                if step == 1:
                    pairs.append((p0, apply(residual, diagonal, off)[8:16]))
                    again = apply(image, diagonal, off)[8:16]
                    pairs += [(p0, again), (q1, again)]
                for k, (p, q) in enumerate(pairs):
                    block = jnp.where(sub == k, jnp.sum(p * q, axis=0, keepdims=True), block)
                sums = jnp.sum(block, axis=1, keepdims=True)
                message = message + jnp.sum(jnp.where(lane == 8 * c + sub, sums, 0.0), axis=0, keepdims=True)
                message = jnp.where((lane1 >= 64 + 8 * c) & (lane1 < 72 + 8 * c), bound, message)
            moment_out[slot] = message
            moment_in[slot, 0] = message

            def send_moments(i, c):
                half = (i + 1) // 2
                moment_copy(slot, tile_n // 2 + jnp.where(i % 2 == 0, half, -half)).start()
                return c

            lax.fori_loop(0, others, send_moments, 0)
            moment_all(slot).wait_recv()
            rows = [moment_in[slot, d] for d in range(tile_n)]
            bounds = [pltpu.roll(m, 64, 1) for m in rows]
            top = functools.reduce(jnp.maximum, bounds)
            inverse = 1.0 / top
            m0 = jnp.zeros((1, LANES), F32)
            for d in range(tile_n):
                m0 = m0 + rows[d] * powers(bounds[d] * inverse)
            m1, m2, m3, m4, m5 = [pltpu.roll(m0, LANES - k, 1) for k in range(1, 6)]
            alpha = m0 / m1
            fresh = jnp.maximum(alpha * alpha * m2 - m0, 0.0)
            beta = fresh / m0
            along = alpha * inverse
            back = alpha * inverse * bounds[0]
            scalars = [along, back, beta]
            if step == 1:
                pivot = m3 - 2.0 * alpha * m4 + alpha * alpha * m5 - beta * beta * m1
                sound = pivot > PIVOT * m3
                scalars.append(jnp.where(sound, fresh / jnp.where(sound, pivot, 1.0), 0.0) * inverse)
            for c in range(3):
                k = [jnp.sum(jnp.where(lane1 == 8 * c, z, 0.0), axis=1, keepdims=True) for z in scalars]
                residual, direction, update = state[c][:3]
                part = k[0] * direction[8:16]
                state[c][0] = residual - k[1] * images[c]
                state[c][1] = state[c][0] + k[2] * direction
                state[c][2] = part if step == 0 else update + part + k[3] * state[c][1][8:16]
        for c in range(3):
            fields_ref[0, c] = state[c][2] if r == 0 else fields_ref[0, c] + state[c][2]

    zero = jnp.zeros((8, LANES), F32)
    carry = lax.fori_loop(0, peers, first_list, (zero,) * 4)
    solve(0, *carry)
    for x in range(rows_x):
        for c in range(3):
            field_rows[x, c:c + 1, :] = fields_ref[0, c, x:x + 1, :]
        field_rows[x, 3:8, :] = jnp.zeros((5, LANES), F32)
    lax.fori_loop(0, peers, send_fields, 0)
    lax.fori_loop(0, rows_x, later_own, 0)
    carry = lax.fori_loop(0, peers, later_list, (zero,) * 4)
    solve(1, *carry)

    def drain(j, c):
        list_copy(j).wait_send()
        field_copy(j).wait_send()
        return c

    lax.fori_loop(0, peers, drain, 0)
    for r in range(ROUNDS):
        edge_copy(0, r).wait_send()
        edge_copy(1, r).wait_send()
        for step in range(SUMS):
            moment_all(r * SUMS + step).wait_send()


def correct_kernel(data_hbm, fields_hbm, fields_out, volume_hbm, data, fields, volume, load_sem, store_sem):
    rows_x, rows_y, samples = data.shape
    parts = load_sem.shape[0] - 1
    rows = rows_x // parts
    lane = lax.broadcasted_iota(jnp.int32, (rows_y, samples), 1)
    time_pos = (lane.astype(F32) - (samples - 1) / 2.0) / (samples / 2.0)
    field_load = pltpu.make_async_copy(fields_hbm, fields, load_sem.at[parts])
    field_load.start()

    def load(k):
        part = pl.ds(k * rows, rows)
        return pltpu.make_async_copy(data_hbm.at[0, part], data.at[part], load_sem.at[k])

    def store(k):
        part = pl.ds(k * rows, rows)
        return pltpu.make_async_copy(volume.at[part], volume_hbm.at[0, part], store_sem.at[k])

    for k in range(parts):
        load(k).start()
    field_load.wait()
    field_store = pltpu.make_async_copy(fields, fields_out, store_sem.at[parts])
    field_store.start()
    columns = [fields[0, c].T for c in range(3)]
    for k in range(parts):
        load(k).wait()
        for x in range(k * rows, (k + 1) * rows):
            shift, log_gain, trend = [column[:, x:x + 1] for column in columns]
            d = data[x].astype(F32)
            after = jnp.where(lane == samples - 1, 0.0, pltpu.roll(d, samples - 1, 1))
            before = jnp.where(lane == 0, 0.0, pltpu.roll(d, 1, 1))
            amplitude = jnp.exp(log_gain + trend * time_pos)
            volume[x] = (amplitude * (d + shift * (0.5 * (after - before)))).astype(BF16)
        store(k).start()
    for k in range(parts):
        store(k).wait()
    field_store.wait()


def correct(data, fields):
    rows_x, rows_y, samples = data.shape[1:]
    parts = 4
    block = pltpu.VMEM((rows_x, rows_y, samples), BF16)
    return pl.pallas_call(
        correct_kernel,
        out_shape=(jax.ShapeDtypeStruct(fields.shape, F32), jax.ShapeDtypeStruct(data.shape, BF16)),
        in_specs=[pl.BlockSpec(memory_space=pl.ANY)] * 2,
        out_specs=[pl.BlockSpec(memory_space=pl.ANY)] * 2,
        scratch_shapes=[block, pltpu.VMEM(fields.shape, F32), block,
                        pltpu.SemaphoreType.DMA((parts + 1,)), pltpu.SemaphoreType.DMA((parts + 1,))],
        compiler_params=pltpu.CompilerParams(vmem_limit_bytes=60 * 1024 * 1024),
    )(data, fields)


def local(data, correlation_index, correlation_count, smoothing):
    survey_n = lax.axis_size("survey")
    tile_n = lax.axis_size("tile")
    rows_x, rows_y, samples = data.shape[1:]
    peers = survey_n - 1
    block = (samples, LANES)
    turned = (LANES, samples)
    dma = pltpu.SemaphoreType.DMA
    fields = pl.pallas_call(
        functools.partial(kernel, survey_n, tile_n),
        out_shape=jax.ShapeDtypeStruct((1, 3, rows_x, rows_y), F32),
        in_specs=[pl.BlockSpec(memory_space=pl.ANY)] * 4,
        out_specs=pl.BlockSpec(memory_space=pltpu.VMEM),
        scratch_shapes=[
            pltpu.VMEM((rows_x,) + turned, BF16),
            pltpu.SMEM((survey_n, correlation_index.shape[3]), jnp.int32),
            pltpu.SMEM((survey_n, correlation_index.shape[3]), jnp.int32),
            pltpu.SMEM(correlation_count.shape, jnp.int32),
            pltpu.SMEM(smoothing.shape, F32),
            pltpu.VMEM((rows_x,) + block, BF16),
            pltpu.VMEM((rows_x,) + block, F32),
            pltpu.VMEM((rows_x,) + block, BF16),
            pltpu.VMEM((rows_x,) + block, F32),
            pltpu.VMEM((5, rows_x, LANES), F32),
            pltpu.VMEM((peers,) + turned, BF16),
            pltpu.VMEM((peers,) + turned, BF16),
            pltpu.VMEM((peers,) + block, BF16),
            pltpu.VMEM((peers,) + block, F32),
            pltpu.VMEM((ROUNDS, 6, rows_x, LANES), F32),
            pltpu.VMEM((ROUNDS, 6, rows_x, LANES), F32),
            pltpu.VMEM((ROUNDS, 6, rows_x, LANES), F32),
            pltpu.VMEM((ROUNDS * SUMS, 1, LANES), F32),
            pltpu.VMEM((ROUNDS * SUMS, tile_n, 1, LANES), F32),
            pltpu.VMEM((rows_x, 8, LANES), F32),
            pltpu.VMEM((peers, 8, LANES), F32),
            pltpu.VMEM((peers, 8, LANES), F32),
            dma((5,)),
            dma((peers,)), dma((peers,)),
            dma((ROUNDS, 2)), dma((ROUNDS, 2)),
            dma((ROUNDS * SUMS,)), dma((ROUNDS * SUMS,)),
            dma((peers,)), dma((peers,)),
        ],
        compiler_params=pltpu.CompilerParams(
            collective_id=0, has_side_effects=True, vmem_limit_bytes=60 * 1024 * 1024),
    )(data, correlation_index, correlation_count, smoothing)
    return correct(data, fields)


def solution(mesh):
    placed = (
        P("survey", "tile", None, None),
        P(None, "tile", None, None),
        P(None, "tile", None),
        P(),
    )
    return jax.shard_map(
        local,
        mesh=mesh,
        in_specs=placed,
        out_specs=(P("survey", None, "tile", None), P("survey", "tile", None, None)),
        check_vma=False,
    )
```

```python
import functools

import jax
import jax.numpy as jnp
from jax import lax
from jax.experimental import pallas as pl
from jax.experimental.pallas import tpu as pltpu
from jax.sharding import PartitionSpec as P

ROUNDS = 2
DAMPING = 0.05
SIM_EPS = 1e-05
CG_ITERS = 3
CHUNK = 32
LANES = 128
F32 = jnp.float32
BF16 = jnp.bfloat16


def slope_of(v):
    n = v.shape[0]
    row = lax.broadcasted_iota(jnp.int32, v.shape, 0)
    after = jnp.where(row == n - 1, 0.0, pltpu.roll(v, n - 1, 0))
    before = jnp.where(row == 0, 0.0, pltpu.roll(v, 1, 0))
    return 0.5 * (after - before)


def time_rows(start, length, samples):
    row = lax.broadcasted_iota(jnp.int32, (length, LANES), 0) + start
    return (row.astype(F32) - (samples - 1) / 2.0) / (samples / 2.0)


def fold(a):
    return jnp.sum(a.reshape(a.shape[0] // 8, 8, a.shape[1]), axis=0)


def kernel(
    survey_n, tile_n, data_hbm, index_hbm, count_hbm, strength_hbm, fields_ref,
    data, send_index, recv_index, count_ref, strength_ref, raw, raw_slope, own, own_slope, stats,
    out_lists, in_lists, list_raw, list_slope,
    edge_out, edge_low, edge_high, moment_out, moment_in, field_rows, field_out, field_in,
    load_sem, list_send, list_recv, edge_send, edge_recv, moment_send, moment_recv, field_send, field_recv,
):
    rows_x, rows_y, samples = data.shape
    me = lax.axis_index("survey")
    tile = lax.axis_index("tile")
    peers = survey_n - 1
    others = tile_n - 1
    lane = lax.broadcasted_iota(jnp.int32, (8, LANES), 1)
    sub = lax.broadcasted_iota(jnp.int32, (8, LANES), 0)
    lane1 = lax.broadcasted_iota(jnp.int32, (1, LANES), 1)

    def offset(j):
        half = (j + 1) // 2
        return jnp.where(j % 2 == 0, half + 1, survey_n - half)

    def receiver(j):
        return lax.rem(me + offset(j), survey_n)

    def sender(j):
        return lax.rem(me + survey_n - offset(j), survey_n)

    loads = [
        pltpu.make_async_copy(index_hbm.at[me, 0], send_index, load_sem.at[0]),
        pltpu.make_async_copy(data_hbm.at[0], data, load_sem.at[1]),
        pltpu.make_async_copy(index_hbm.at[:, 0, me], recv_index, load_sem.at[2]),
        pltpu.make_async_copy(count_hbm, count_ref, load_sem.at[3]),
        pltpu.make_async_copy(strength_hbm, strength_ref, load_sem.at[4]),
    ]
    for load in loads:
        load.start()
    barrier = pltpu.get_barrier_semaphore()

    def greet_survey(i, c):
        pl.semaphore_signal(barrier, inc=1, device_id={"survey": lax.rem(me + i, survey_n)},
                            device_id_type=pl.DeviceIdType.MESH)
        return c

    def greet_tile(i, c):
        pl.semaphore_signal(barrier, inc=1, device_id={"tile": lax.rem(tile + i, tile_n)},
                            device_id_type=pl.DeviceIdType.MESH)
        return c

    lax.fori_loop(1, survey_n, greet_survey, 0)
    lax.fori_loop(1, tile_n, greet_tile, 0)
    loads[0].wait()
    loads[1].wait()

    def list_copy(j):
        return pltpu.make_async_remote_copy(
            src_ref=out_lists.at[j], dst_ref=in_lists.at[j], send_sem=list_send.at[j],
            recv_sem=list_recv.at[j], device_id={"survey": receiver(j)},
            device_id_type=pl.DeviceIdType.MESH)

    def build_list(j):
        start = send_index[receiver(j), 0]
        x0 = start // LANES
        y0 = start % LANES
        x1 = jnp.minimum(x0 + 1, rows_x - 1)
        for y in range(0, rows_y, CHUNK):
            place = lax.broadcasted_iota(jnp.int32, (CHUNK, samples), 0) + y
            first = place.astype(F32).astype(BF16) >= jnp.full((CHUNK, samples), y0, jnp.int32).astype(F32).astype(BF16)
            out_lists[j, y:y + CHUNK, :] = jnp.where(first, data[x0, y:y + CHUNK, :], data[x1, y:y + CHUNK, :])

    build_list(0)
    pl.semaphore_wait(barrier, peers + others)
    list_copy(0).start()

    def send_list(j, c):
        build_list(j)
        list_copy(j).start()
        return c

    lax.fori_loop(1, peers, send_list, 0)
    for load in loads[2:]:
        load.wait()

    def row_stats(x, slopes, values):
        sums = [jnp.zeros((8, LANES), F32) for _ in range(5)]
        for t in range(0, samples, CHUNK):
            u = values[x, t:t + CHUNK, :].astype(F32)
            a = slopes[x, t:t + CHUNK, :]
            w = u * time_rows(t, CHUNK, samples)
            for k, (p, q) in enumerate(((u, u), (a, a), (w, w), (u, a), (u, w))):
                sums[k] = sums[k] + fold(p * q)
        for k in range(5):
            stats[k, pl.ds(x, 1), :] = jnp.sum(sums[k], axis=0, keepdims=True) * (1.0 / samples)

    def first_own(x, c):
        raw[x] = data[x].T
        raw_slope[x] = slope_of(raw[x].astype(F32))
        row_stats(x, raw_slope, raw)
        return c

    lax.fori_loop(0, rows_x, first_own, 0)

    def later_own(x, c):
        shift = fields_ref[0, 0, pl.ds(x, 1), :]
        log_gain = fields_ref[0, 1, pl.ds(x, 1), :]
        trend = fields_ref[0, 2, pl.ds(x, 1), :]
        for t in range(0, samples, CHUNK):
            amplitude = jnp.exp(log_gain + trend * time_rows(t, CHUNK, samples))
            d = raw[x, t:t + CHUNK, :].astype(F32)
            own[x, t:t + CHUNK, :] = (amplitude * (d + shift * raw_slope[x, t:t + CHUNK, :])).astype(BF16)
        own_slope[x] = slope_of(own[x].astype(F32))
        row_stats(x, own_slope, own)
        return c

    def list_terms(j, carry, values, slopes, partner):
        total, t0, t1, t2 = carry
        source = sender(j)
        start = recv_index[source, 0]
        count = count_ref[source, 0, me]
        x0 = start // LANES
        y0 = start % LANES
        x1 = jnp.minimum(x0 + 1, rows_x - 1)
        y = lax.broadcasted_iota(jnp.int32, (CHUNK, LANES), 1)
        first = y >= y0
        sums = [jnp.zeros((8, LANES), F32) for _ in range(4)]
        for t in range(0, samples, CHUNK):
            v = partner(j, t)
            u = jnp.where(first, values[x0, t:t + CHUNK, :], values[x1, t:t + CHUNK, :]).astype(F32)
            a = jnp.where(first, slopes[x0, t:t + CHUNK, :], slopes[x1, t:t + CHUNK, :])
            uv = u * v
            sums[0] = sums[0] + fold(uv)
            sums[1] = sums[1] + fold(a * v)
            sums[2] = sums[2] + fold(uv * time_rows(t, CHUNK, samples))
            sums[3] = sums[3] + fold(v * v)
        uv, av, wv, vv = [jnp.sum(s, axis=0, keepdims=True) * (1.0 / samples) for s in sums]
        slot = sub * LANES + lane - start
        live = (slot >= 0) & (slot < count)
        uu = stats[0]
        weight = jnp.where(live, (uv * uv) / ((uu + SIM_EPS) * (vv + SIM_EPS)), 0.0)
        return (total + weight, t0 + weight * (av - stats[3]), t1 + weight * (uv - uu),
                t2 + weight * (wv - stats[4]))

    def first_list(j, carry):
        list_copy(j).wait_recv()
        d = in_lists[j].T
        list_raw[j] = d
        return list_terms(j, carry, raw, raw_slope, lambda j, t: list_raw[j, t:t + CHUNK, :].astype(F32))

    def later_partner(j, t):
        shift = field_in[j, 0:1, :]
        log_gain = field_in[j, 1:2, :]
        trend = field_in[j, 2:3, :]
        amplitude = jnp.exp(log_gain + trend * time_rows(t, CHUNK, samples))
        d = list_raw[j, t:t + CHUNK, :].astype(F32)
        return (amplitude * (d + shift * list_slope[j, t:t + CHUNK, :])).astype(BF16).astype(F32)

    def field_copy(j):
        return pltpu.make_async_remote_copy(
            src_ref=field_out.at[j], dst_ref=field_in.at[j], send_sem=field_send.at[j],
            recv_sem=field_recv.at[j], device_id={"survey": receiver(j)},
            device_id_type=pl.DeviceIdType.MESH)

    def later_list(j, carry):
        field_copy(j).wait_recv()
        return list_terms(j, carry, own, own_slope, later_partner)

    def send_fields(i, c):
        j = peers - 1 - i
        start = send_index[receiver(j), 0]
        x0 = start // LANES
        y0 = start % LANES
        x1 = jnp.minimum(x0 + 1, rows_x - 1)
        field_out[j] = jnp.where(lane[0:4] >= y0, field_rows[x0], field_rows[x1])
        field_copy(j).start()
        return c

    def edge_copy(side, r):
        step = 1 if side == 0 else tile_n - 1
        return pltpu.make_async_remote_copy(
            src_ref=edge_out.at[r], dst_ref=(edge_low if side == 0 else edge_high).at[r],
            send_sem=edge_send.at[r, side], recv_sem=edge_recv.at[r, side],
            device_id={"tile": lax.rem(tile + step, tile_n)}, device_id_type=pl.DeviceIdType.MESH)

    def moment_copy(r, d):
        return pltpu.make_async_remote_copy(
            src_ref=moment_out.at[r], dst_ref=moment_in.at[r, d],
            send_sem=moment_send.at[r], recv_sem=moment_recv.at[r],
            device_id={"tile": lax.rem(tile + d, tile_n)}, device_id_type=pl.DeviceIdType.MESH)

    def moment_all(r):
        return pltpu.make_async_remote_copy(
            src_ref=moment_in.at[r, pl.ds(1, others)], dst_ref=moment_in.at[r, pl.ds(1, others)],
            send_sem=moment_send.at[r], recv_sem=moment_recv.at[r],
            device_id={"tile": lax.rem(tile + 1, tile_n)}, device_id_type=pl.DeviceIdType.MESH)

    def slope_list(j, c):
        list_slope[j] = slope_of(list_raw[j].astype(F32))
        return c

    def solve(r, total, t0, t1, t2):
        for c, t in enumerate((t0, t1, t2)):
            edge_out[r, c] = t
        edge_out[r, 3] = total * stats[1]
        edge_out[r, 4] = total * stats[0]
        edge_out[r, 5] = total * stats[2]
        edge_copy(0, r).start()
        edge_copy(1, r).start()
        if r == 0:
            lax.fori_loop(0, peers, slope_list, 0)
        edge_copy(0, r).wait_recv()
        edge_copy(1, r).wait_recv()

        row = lax.broadcasted_iota(jnp.int32, (24, LANES), 0)
        col = lax.broadcasted_iota(jnp.int32, (24, LANES), 1)
        inside = ((row >= 8) | (tile > 0)) & ((row < 16) | (tile < tile_n - 1))
        state = []
        for c in range(3):
            strength = strength_ref[c]
            b = jnp.where(inside, jnp.concatenate([edge_low[r, c], edge_out[r, c], edge_high[r, c]], axis=0), 0.0)
            w = jnp.where(inside, jnp.concatenate(
                [edge_low[r, 3 + c], edge_out[r, 3 + c], edge_high[r, 3 + c]], axis=0), 0.0)
            bound = jnp.max(jnp.max(w, axis=0, keepdims=True), axis=1, keepdims=True) + (DAMPING + 8.0 * strength)
            scale = 1.0 / bound
            diagonal = (w + DAMPING + 4.0 * strength) * scale
            state.append([b, b, None, bound, diagonal, strength * scale])

        def apply(y, diagonal, off):
            up = pltpu.roll(y, 1, 0)
            down = pltpu.roll(y, 23, 0)
            left = jnp.where(col == 0, 0.0, pltpu.roll(y, 1, 1))
            right = jnp.where(col == LANES - 1, 0.0, pltpu.roll(y, LANES - 1, 1))
            return jnp.where(inside, diagonal * y - off * (up + down + left + right), 0.0)

        power = lane1 % 8

        def powers(q):
            return jnp.where(power == 1, q, 1.0) * jnp.where(power == 2, q * q, 1.0)

        for step in range(CG_ITERS):
            slot = r * CG_ITERS + step
            message = jnp.where(lane1 >= 64, 1.0, 0.0).astype(F32)
            images = []
            for c in range(3):
                residual, direction, update, bound, diagonal, off = state[c]
                image = apply(direction, diagonal, off)
                images.append(image)
                p0, p1, q1 = residual[8:16], direction[8:16], image[8:16]
                block = jnp.zeros((8, LANES), F32)
                for k, (p, q) in enumerate(((p0, p0), (p1, q1), (q1, q1))):
                    block = jnp.where(sub == k, jnp.sum(p * q, axis=0, keepdims=True), block)
                sums = jnp.sum(block, axis=1, keepdims=True)
                message = message + jnp.sum(jnp.where(lane == 8 * c + sub, sums, 0.0), axis=0, keepdims=True)
                message = jnp.where((lane1 >= 64 + 8 * c) & (lane1 < 72 + 8 * c), bound, message)
            moment_out[slot] = message
            moment_in[slot, 0] = message

            def send_moments(i, c):
                half = (i + 1) // 2
                moment_copy(slot, tile_n // 2 + jnp.where(i % 2 == 0, half, -half)).start()
                return c

            lax.fori_loop(0, others, send_moments, 0)
            moment_all(slot).wait_recv()
            rows = [moment_in[slot, d] for d in range(tile_n)]
            bounds = [pltpu.roll(m, 64, 1) for m in rows]
            top = functools.reduce(jnp.maximum, bounds)
            inverse = 1.0 / top
            m0 = jnp.zeros((1, LANES), F32)
            for d in range(tile_n):
                m0 = m0 + rows[d] * powers(bounds[d] * inverse)
            m1, m2 = [pltpu.roll(m0, LANES - k, 1) for k in (1, 2)]
            alpha = m0 / m1
            beta = jnp.maximum(alpha * alpha * m2 - m0, 0.0) / m0
            along = alpha * inverse
            back = alpha * inverse * bounds[0]
            for c in range(3):
                k1, k2, k3 = [jnp.sum(jnp.where(lane1 == 8 * c, z, 0.0), axis=1, keepdims=True)
                              for z in (along, back, beta)]
                residual, direction, update = state[c][:3]
                part = k1 * direction[8:16]
                state[c][2] = part if step == 0 else update + part
                state[c][0] = residual - k2 * images[c]
                state[c][1] = state[c][0] + k3 * direction
        for c in range(3):
            fields_ref[0, c] = state[c][2] if r == 0 else fields_ref[0, c] + state[c][2]

    zero = jnp.zeros((8, LANES), F32)
    carry = lax.fori_loop(0, peers, first_list, (zero,) * 4)
    solve(0, *carry)
    for x in range(rows_x):
        for c in range(3):
            field_rows[x, c:c + 1, :] = fields_ref[0, c, x:x + 1, :]
        field_rows[x, 3:4, :] = jnp.zeros((1, LANES), F32)
    lax.fori_loop(0, peers, send_fields, 0)
    lax.fori_loop(0, rows_x, later_own, 0)
    carry = lax.fori_loop(0, peers, later_list, (zero,) * 4)
    solve(1, *carry)

    def drain(j, c):
        list_copy(j).wait_send()
        field_copy(j).wait_send()
        return c

    lax.fori_loop(0, peers, drain, 0)
    for r in range(ROUNDS):
        edge_copy(0, r).wait_send()
        edge_copy(1, r).wait_send()
        for step in range(CG_ITERS):
            moment_all(r * CG_ITERS + step).wait_send()


def correct_kernel(data_hbm, fields_hbm, fields_out, volume_hbm, data, fields, volume, load_sem, store_sem):
    rows_x, rows_y, samples = data.shape
    parts = load_sem.shape[0] - 1
    rows = rows_x // parts
    lane = lax.broadcasted_iota(jnp.int32, (rows_y, samples), 1)
    time_pos = (lane.astype(F32) - (samples - 1) / 2.0) / (samples / 2.0)
    field_load = pltpu.make_async_copy(fields_hbm, fields, load_sem.at[parts])
    field_load.start()

    def load(k):
        part = pl.ds(k * rows, rows)
        return pltpu.make_async_copy(data_hbm.at[0, part], data.at[part], load_sem.at[k])

    def store(k):
        part = pl.ds(k * rows, rows)
        return pltpu.make_async_copy(volume.at[part], volume_hbm.at[0, part], store_sem.at[k])

    for k in range(parts):
        load(k).start()
    field_load.wait()
    field_store = pltpu.make_async_copy(fields, fields_out, store_sem.at[parts])
    field_store.start()
    columns = [fields[0, c].T for c in range(3)]
    for k in range(parts):
        load(k).wait()
        for x in range(k * rows, (k + 1) * rows):
            shift, log_gain, trend = [column[:, x:x + 1] for column in columns]
            d = data[x].astype(F32)
            after = jnp.where(lane == samples - 1, 0.0, pltpu.roll(d, samples - 1, 1))
            before = jnp.where(lane == 0, 0.0, pltpu.roll(d, 1, 1))
            amplitude = jnp.exp(log_gain + trend * time_pos)
            volume[x] = (amplitude * (d + shift * (0.5 * (after - before)))).astype(BF16)
        store(k).start()
    for k in range(parts):
        store(k).wait()
    field_store.wait()


def correct(data, fields):
    rows_x, rows_y, samples = data.shape[1:]
    parts = 4
    block = pltpu.VMEM((rows_x, rows_y, samples), BF16)
    return pl.pallas_call(
        correct_kernel,
        out_shape=(jax.ShapeDtypeStruct(fields.shape, F32), jax.ShapeDtypeStruct(data.shape, BF16)),
        in_specs=[pl.BlockSpec(memory_space=pl.ANY)] * 2,
        out_specs=[pl.BlockSpec(memory_space=pl.ANY)] * 2,
        scratch_shapes=[block, pltpu.VMEM(fields.shape, F32), block,
                        pltpu.SemaphoreType.DMA((parts + 1,)), pltpu.SemaphoreType.DMA((parts + 1,))],
        compiler_params=pltpu.CompilerParams(vmem_limit_bytes=60 * 1024 * 1024),
    )(data, fields)


def local(data, correlation_index, correlation_count, smoothing):
    survey_n = lax.axis_size("survey")
    tile_n = lax.axis_size("tile")
    rows_x, rows_y, samples = data.shape[1:]
    peers = survey_n - 1
    block = (samples, LANES)
    turned = (LANES, samples)
    dma = pltpu.SemaphoreType.DMA
    fields = pl.pallas_call(
        functools.partial(kernel, survey_n, tile_n),
        out_shape=jax.ShapeDtypeStruct((1, 3, rows_x, rows_y), F32),
        in_specs=[pl.BlockSpec(memory_space=pl.ANY)] * 4,
        out_specs=pl.BlockSpec(memory_space=pltpu.VMEM),
        scratch_shapes=[
            pltpu.VMEM((rows_x,) + turned, BF16),
            pltpu.SMEM((survey_n, correlation_index.shape[3]), jnp.int32),
            pltpu.SMEM((survey_n, correlation_index.shape[3]), jnp.int32),
            pltpu.SMEM(correlation_count.shape, jnp.int32),
            pltpu.SMEM(smoothing.shape, F32),
            pltpu.VMEM((rows_x,) + block, BF16),
            pltpu.VMEM((rows_x,) + block, F32),
            pltpu.VMEM((rows_x,) + block, BF16),
            pltpu.VMEM((rows_x,) + block, F32),
            pltpu.VMEM((5, rows_x, LANES), F32),
            pltpu.VMEM((peers,) + turned, BF16),
            pltpu.VMEM((peers,) + turned, BF16),
            pltpu.VMEM((peers,) + block, BF16),
            pltpu.VMEM((peers,) + block, F32),
            pltpu.VMEM((ROUNDS, 6, rows_x, LANES), F32),
            pltpu.VMEM((ROUNDS, 6, rows_x, LANES), F32),
            pltpu.VMEM((ROUNDS, 6, rows_x, LANES), F32),
            pltpu.VMEM((ROUNDS * CG_ITERS, 1, LANES), F32),
            pltpu.VMEM((ROUNDS * CG_ITERS, tile_n, 1, LANES), F32),
            pltpu.VMEM((rows_x, 4, LANES), F32),
            pltpu.VMEM((peers, 4, LANES), F32),
            pltpu.VMEM((peers, 4, LANES), F32),
            dma((5,)),
            dma((peers,)), dma((peers,)),
            dma((ROUNDS, 2)), dma((ROUNDS, 2)),
            dma((ROUNDS * CG_ITERS,)), dma((ROUNDS * CG_ITERS,)),
            dma((peers,)), dma((peers,)),
        ],
        compiler_params=pltpu.CompilerParams(
            collective_id=0, has_side_effects=True, vmem_limit_bytes=60 * 1024 * 1024),
    )(data, correlation_index, correlation_count, smoothing)
    return correct(data, fields)


def solution(mesh):
    placed = (
        P("survey", "tile", None, None),
        P(None, "tile", None, None),
        P(None, "tile", None),
        P(),
    )
    return jax.shard_map(
        local,
        mesh=mesh,
        in_specs=placed,
        out_specs=(P("survey", None, "tile", None), P("survey", "tile", None, None)),
        check_vma=False,
    )
```
